32 devices in a mesh: rows: 8 (over y, x, core), cols: 4 (over z).
Axes of the slice: x: 2, y: 2, z: 4, core: 2. Of those that a mesh axis runs over, the one named last changes fastest.
Arguments:
- features: bfloat16 [5120, 1152], P('rows', 'cols'), may hold values from -6 to 6
- weight: bfloat16 [1152, 1152], replicated, may hold values from -0.1875 to 0.1875
- bias: float32 [1152], P('cols'), may hold values from -3 to 3
- tile_values: bfloat16 [40, 48, 128, 128], P('rows'), may hold values from -0.078125 to 0.078125
- tile_coords: int32 [40, 48], P('rows'), may hold values from 0 to 39, as said below
- tile_counts: int32 [40], P('rows'), may hold values from 1 to 48, as said below
- cotangent: bfloat16 [5120, 1152], P('rows', 'cols'), may hold values from -6 to 6
Outputs:
- activations: bfloat16 [5120, 1152], P('rows', 'cols')
- input_grad: bfloat16 [5120, 1152], P('rows', 'cols')
- weight_grad: float32 [1152, 1152], P('rows', 'cols')
The draws below stay inside these ranges and needn't reach their ends.
Inputs may be any that keep to these rules, and one draw needn't show every extreme that they name: `tile_counts`: each row block has between 1 and 48 live slots, and some row block has exactly 48; slots at or beyond the count are ignored. `tile_coords`: source row block of each tile slot; a block may appear in several slots.
All inputs are finite; a program needn't handle non-finite values.
Results may differ from the reference program's by a relative error of at most 0.006.
Values may be sent and summed in bfloat16 or wider, within the bound.
No kernel may reach another device: no remote copies, remote signals or barrier semaphores. Data moves between devices by JAX's collectives and lax.ppermute only.
A program may use at most 128 MiB of HBM per device.

```python
import math
import jax
import jax.numpy as jnp
from jax import lax

F = 1152
TILE = 128
K = 48
RB_DEV = 5
BLOCKS = 40
NODES = 5120
N_ROWS = 8


def draw_tile_counts(key, part):
    first, second, third = jax.random.split(key, 3)
    lowest = max(1, K // 12)
    highest = max(lowest + 1, K // 3 + 1)
    base = jax.random.randint(first, (BLOCKS,), lowest, highest)
    heavy = jax.random.randint(second, (BLOCKS,), 0, 4) == 0
    counts = jnp.where(heavy, K, base)
    chosen = jax.random.randint(third, (), 0, BLOCKS)
    counts = jnp.where(jnp.arange(BLOCKS) == chosen, K, counts)
    return counts.astype(jnp.int32)


def draw_tile_coords(key, part):
    first, second, third = jax.random.split(jax.random.fold_in(key, 7), 3)
    near = jax.random.randint(first, (BLOCKS, K), -8, 9)
    far = jax.random.randint(second, (BLOCKS, K), 0, BLOCKS)
    distant = jax.random.randint(third, (BLOCKS, K), 0, 2) == 0
    own = jnp.arange(BLOCKS, dtype=jnp.int32)[:, None]
    coords = jnp.where(distant, far, jnp.mod(own + near, BLOCKS))
    coords = jnp.where(jnp.arange(K)[None, :] == 0, own, coords)
    return coords.astype(jnp.int32)


def steps_of(rng, shape, pieces, smallest, high):
    gain = 1.0
    for axis_at, parts in pieces:
        draws = jax.random.uniform(jax.random.fold_in(jax.random.fold_in(rng, 6), axis_at), (parts,), jnp.float32, smallest / len(pieces), high / len(pieces))
        gain = gain * jnp.repeat(jnp.exp(draws), shape[axis_at] // parts).reshape((-1,) + (1,) * (len(shape) - 1 - axis_at))
    return gain


def gaussian(stream_key, shape, width, reach, cuts=(), kind=jnp.bfloat16):
    values = jax.random.normal(stream_key, shape, jnp.float32) * width
    if len(cuts) > 0:
        values = steps_of(stream_key, shape, cuts, -0.22, 0.18) * values
    return jnp.clip(values, min=-reach, max=reach).astype(kind)


def setup_inputs(seed: int = 0) -> dict:
    seeds = jax.random.split(jax.random.key(seed), 8)
    features = gaussian(seeds[0], (NODES, F), 1.0, 6.0, ((0, 8), (1, 4)))
    weight = gaussian(seeds[1], (F, F), F ** -0.5, 0.1875)
    bias = gaussian(seeds[2], (F,), 0.5, 3.0, ((0, 4),), jnp.float32)
    tile_values = gaussian(seeds[3], (BLOCKS, K, TILE, TILE), (K * TILE) ** -0.5, 0.078125, ((0, 8),))
    tile_coords = draw_tile_coords(jax.random.fold_in(seeds[7], 71), 0)
    tile_counts = draw_tile_counts(jax.random.fold_in(seeds[7], 71), 0)
    cotangent = gaussian(seeds[6], (NODES, F), 1.0, 6.0, ((0, 8), (1, 4)))
    return {"features": features, "weight": weight, "bias": bias, "tile_values": tile_values, "tile_coords": tile_coords, "tile_counts": tile_counts, "cotangent": cotangent}


def silu_slope(v):
    s = jax.nn.sigmoid(v)
    return s * (1.0 + v * (1.0 - s))

def reference(features, weight, bias, tile_values, tile_coords, tile_counts, cotangent):
    hidden = jnp.dot(features, weight, preferred_element_type=jnp.float32).astype(jnp.bfloat16)
    blocks_hidden = hidden.reshape(BLOCKS, TILE, F)
    slot_ids = jnp.arange(K, dtype=jnp.int32)
    live = slot_ids[None, :] < tile_counts[:, None]
    index = jnp.where(live, tile_coords, BLOCKS).astype(jnp.int32)

    def one_block(args):
        values, idx = args
        panels = blocks_hidden.at[idx].get(mode='fill', fill_value=0)
        return jnp.einsum('kij,kjf->if', values.astype(jnp.float32), panels.astype(jnp.float32))
    aggregated = lax.map(one_block, (tile_values, index)).reshape(NODES, F)
    pre = aggregated + bias[None, :]
    activations = jax.nn.silu(pre).astype(jnp.bfloat16)
    grad_pre = (cotangent.astype(jnp.float32) * silu_slope(pre)).astype(jnp.bfloat16)
    group_values = tile_values.reshape(N_ROWS, RB_DEV, K, TILE, TILE)
    group_grad = grad_pre.reshape(N_ROWS, RB_DEV, TILE, F)
    group_index = index.reshape(N_ROWS, RB_DEV * K)

    def one_group(total, args):
        values, grads, idx = args
        contrib = jnp.einsum('bkij,bif->bkjf', values.astype(jnp.float32), grads.astype(jnp.float32))
        buffer = jnp.zeros((BLOCKS, TILE, F), jnp.float32).at[idx].add(contrib.reshape(RB_DEV * K, TILE, F), mode='drop')
        return (total + buffer, None)
    total, unused = lax.scan(one_group, jnp.zeros((BLOCKS, TILE, F), jnp.float32), (group_values, group_grad, group_index))
    grad_hidden = total.reshape(NODES, F).astype(jnp.bfloat16)
    input_grad = jnp.dot(grad_hidden, weight.T, preferred_element_type=jnp.float32).astype(jnp.bfloat16)
    weight_grad = jnp.dot(features.T, grad_hidden, preferred_element_type=jnp.float32) * (1.0 / math.sqrt(NODES))
    return (activations, input_grad, weight_grad)
```

```python
import functools
import math

import jax
import jax.numpy as jnp
from jax import lax
from jax.experimental import pallas as pl
from jax.experimental.pallas import tpu as pltpu
from jax.sharding import PartitionSpec as P

F32 = jnp.float32
BF16 = jnp.bfloat16


def largest_divisor(number, limit):
    return max(d for d in range(1, limit + 1) if number % d == 0)


def tile_kernel(
    block_count,
    slots,
    tile,
    group,
    shard_order,
    coords_ref,
    counts_ref,
    me_ref,
    bias_ref,
    cotangent_ref,
    tiles_ref,
    *rest,
):
    shards = len(shard_order)
    hidden_refs = rest[:shards]
    act_ref, part_ref, tiles, hidden, partial, tile_sems, hidden_sems = rest[shards:]
    groups = slots // group
    me = me_ref[0]

    def tile_copy(i, q):
        span = pl.ds(q * group, group)
        return pltpu.make_async_copy(
            tiles_ref.at[i, span], tiles.at[i, span], tile_sems.at[i, q]
        )

    def hidden_copy(s, b):
        owner = me ^ shard_order[s]
        return pltpu.make_async_copy(
            hidden_refs[s].at[:, pl.ds(b * tile, tile)],
            hidden.at[owner * block_count + b],
            hidden_sems.at[s, b],
        )

    for s in range(shards):
        for b in range(block_count):
            hidden_copy(s, b).start()
    for i in range(block_count):
        for q in range(groups):

            @pl.when(q * group < counts_ref[i])
            def _():
                tile_copy(i, q).start()

    partial[...] = jnp.zeros_like(partial)
    for s in range(shards):
        for b in range(block_count):
            hidden_copy(s, b).wait()

    def pair(i, p):
        first = 2 * p
        second = jnp.minimum(first + 1, slots - 1)
        left = tiles[i, first]
        right = tiles[i, second]
        right = jnp.where(first + 1 < counts_ref[i], right, jnp.zeros_like(right))
        both = jnp.concatenate([left, right], axis=1)
        return both, coords_ref[i * slots + first], coords_ref[i * slots + second]

    for i in range(block_count):
        for q in range(groups):

            @pl.when(q * group < counts_ref[i])
            def _():
                tile_copy(i, q).wait()

        pairs = (counts_ref[i] + 1) // 2
        lanes = pl.ds(i * tile, tile)

        def forward(p, total):
            both, c0, c1 = pair(i, p)
            panel = jnp.concatenate([hidden[c0], hidden[c1]], axis=1)
            return total + lax.dot_general(
                panel, both, (((1,), (1,)), ((), ())), preferred_element_type=F32
            )

        width = act_ref.shape[0]
        total = lax.fori_loop(0, pairs, forward, jnp.zeros((width, tile), F32))
        pre = total + bias_ref[...]
        s = jax.nn.sigmoid(pre)
        act_ref[:, lanes] = (pre * s).astype(BF16)
        slope = s * (1.0 + pre * (1.0 - s))
        grad = (cotangent_ref[:, lanes].astype(F32) * slope).astype(BF16)

        def backward(p, carry):
            both, c0, c1 = pair(i, p)
            out = jnp.dot(grad, both, preferred_element_type=F32)
            partial[c0] += out[:, :tile]
            partial[c1] += out[:, tile:]
            return carry

        lax.fori_loop(0, pairs, backward, 0)

    for s in range(shards):
        owner = me ^ shard_order[s]
        for b in range(block_count):
            part_ref[s, :, b * tile : (b + 1) * tile] = partial[owner * block_count + b].astype(BF16)


def tile_products(shard_order, hidden, coords, counts, me, bias, cotangent, tiles):
    block_count, slots, tile, unused_side = tiles.shape
    width, rows_dev = hidden[0].shape
    shards = len(shard_order)
    group = largest_divisor(slots, 8)
    smem = pl.BlockSpec(memory_space=pltpu.SMEM)
    vmem = pl.BlockSpec(memory_space=pltpu.VMEM)
    hbm = pl.BlockSpec(memory_space=pl.ANY)
    flops = 4 * block_count * slots * tile * tile * width
    return pl.pallas_call(
        functools.partial(tile_kernel, block_count, slots, tile, group, shard_order),
        out_shape=(
            jax.ShapeDtypeStruct((width, rows_dev), BF16),
            jax.ShapeDtypeStruct((shards, width, rows_dev), BF16),
        ),
        in_specs=[smem, smem, smem, vmem, vmem, hbm] + [hbm] * shards,
        out_specs=(vmem, vmem),
        scratch_shapes=[
            pltpu.VMEM(tiles.shape, BF16),
            pltpu.VMEM((shards * block_count, width, tile), BF16),
            pltpu.VMEM((shards * block_count, width, tile), F32),
            pltpu.SemaphoreType.DMA((block_count, slots // group)),
            pltpu.SemaphoreType.DMA((shards, block_count)),
        ],
        compiler_params=pltpu.CompilerParams(vmem_limit_bytes=48 * 1024 * 1024),
        cost_estimate=pl.CostEstimate(
            flops=flops, bytes_accessed=2 * tiles.size, transcendentals=width * rows_dev
        ),
    )(coords.reshape(-1), counts, me.reshape(1), bias[:, None], cotangent, tiles, *hidden)


def contract_first(a, b):
    return lax.dot_general(a, b, (((0,), (0,)), ((), ())), preferred_element_type=F32)


def local(features, weight, bias, tile_values, tile_coords, tile_counts, cotangent):
    rows_dev, col_width = features.shape
    n_rows = lax.axis_size("rows")
    me = lax.axis_index("rows")
    col_start = lax.axis_index("cols") * col_width
    x_full = lax.all_gather(features.T, "cols", axis=0, tiled=True)
    w_cols = lax.dynamic_slice_in_dim(weight, col_start, col_width, 1)
    hidden = contract_first(w_cols, x_full).astype(BF16)
    all_hidden = lax.all_gather(hidden, "rows", axis=0)
    order = tuple(range(n_rows))
    zero = jnp.zeros((), jnp.int32)
    act, part = tile_products(
        order,
        [all_hidden[s] for s in order],
        tile_coords,
        tile_counts,
        zero,
        bias,
        cotangent.T,
        tile_values,
    )
    grad_hidden = lax.psum_scatter(part, "rows", scatter_dimension=0, tiled=False)
    w_rows = lax.dynamic_slice_in_dim(weight, col_start, col_width, 0)
    grad_full = lax.all_gather(grad_hidden, "cols", axis=0, tiled=True)
    input_grad = jnp.dot(w_rows, grad_full, preferred_element_type=F32).astype(BF16)
    scale_factor = 1.0 / math.sqrt(rows_dev * n_rows)
    weight_part = lax.dot_general(
        x_full, grad_hidden, (((1,), (1,)), ((), ())), preferred_element_type=F32
    )
    weight_grad = lax.psum_scatter(
        weight_part * scale_factor, "rows", scatter_dimension=0, tiled=True
    )
    return (act.T, input_grad.T, weight_grad)


def solution(mesh):
    return jax.shard_map(
        local,
        mesh=mesh,
        in_specs=(
            P("rows", "cols"),
            P(),
            P("cols"),
            P("rows", None, None, None),
            P("rows", None),
            P("rows"),
            P("rows", "cols"),
        ),
        out_specs=(P("rows", "cols"), P("rows", "cols"), P("rows", "cols")),
        check_vma=False,
    )
```

```python
import functools
import math

import jax
import jax.numpy as jnp
from jax import lax
from jax.experimental import pallas as pl
from jax.experimental.pallas import tpu as pltpu
from jax.sharding import PartitionSpec as P

F32 = jnp.float32
BF16 = jnp.bfloat16
CHUNK = 16


def largest_divisor(number, limit):
    return max(d for d in range(1, limit + 1) if number % d == 0)


def tile_kernel(
    block_count,
    slots,
    tile,
    group,
    shard_order,
    coords_ref,
    counts_ref,
    me_ref,
    bias_ref,
    cotangent_ref,
    tiles_ref,
    *rest,
):
    shards = len(shard_order)
    hidden_refs = rest[:shards]
    act_ref, keep_ref, send_ref, tiles, hidden, partial, tile_sems, hidden_sems = rest[shards:]
    groups = slots // group
    me = me_ref[0]

    def tile_copy(i, q):
        span = pl.ds(q * group, group)
        return pltpu.make_async_copy(
            tiles_ref.at[i, span], tiles.at[i, span], tile_sems.at[i, q]
        )

    def hidden_copy(s, b):
        owner = me ^ shard_order[s]
        return pltpu.make_async_copy(
            hidden_refs[s].at[:, pl.ds(b * tile, tile)],
            hidden.at[owner * block_count + b],
            hidden_sems.at[s, b],
        )

    for s in range(shards):
        for b in range(block_count):
            hidden_copy(s, b).start()
    for i in range(block_count):
        for q in range(groups):

            @pl.when(q * group < counts_ref[i])
            def _():
                tile_copy(i, q).start()

    partial[...] = jnp.zeros_like(partial)
    for s in range(shards):
        for b in range(block_count):
            hidden_copy(s, b).wait()

    chunk = largest_divisor(slots, CHUNK)

    def several(i, p):
        parts, places = [], []
        for t in range(chunk):
            k = p * chunk + t
            value = tiles[i, k]
            if t:
                value = jnp.where(k < counts_ref[i], value, jnp.zeros_like(value))
            parts.append(value)
            places.append(coords_ref[i * slots + k])
        return jnp.concatenate(parts, axis=1), places

    for i in range(block_count):
        for q in range(groups):

            @pl.when(q * group < counts_ref[i])
            def _():
                tile_copy(i, q).wait()

        steps = (counts_ref[i] + (chunk - 1)) // chunk
        lanes = pl.ds(i * tile, tile)

        def forward(p, total):
            values, places = several(i, p)
            panel = jnp.concatenate([hidden[c] for c in places], axis=1)
            return total + lax.dot_general(
                panel, values, (((1,), (1,)), ((), ())), preferred_element_type=F32
            )

        width = act_ref.shape[0]
        total = lax.fori_loop(0, steps, forward, jnp.zeros((width, tile), F32))
        pre = total + bias_ref[...]
        s = jax.nn.sigmoid(pre)
        act_ref[:, lanes] = (pre * s).astype(BF16)
        slope = s * (1.0 + pre * (1.0 - s))
        grad = (cotangent_ref[:, lanes].astype(F32) * slope).astype(BF16)

        def backward(p, carry):
            values, places = several(i, p)
            out = jnp.dot(grad, values, preferred_element_type=F32)
            for t, c in enumerate(places):
                partial[c] += out[:, t * tile : (t + 1) * tile]
            return carry

        lax.fori_loop(0, steps, backward, 0)

    for s in range(shards):
        owner = me ^ shard_order[s]
        half = shards // 2
        out_ref = keep_ref.at[s] if s < half else send_ref.at[s - half]
        for b in range(block_count):
            value = partial[owner * block_count + b].astype(BF16)
            out_ref[:, b * tile : (b + 1) * tile] = value


def tile_products(shard_order, hidden, coords, counts, me, bias, cotangent, tiles):
    block_count, slots, tile, unused_side = tiles.shape
    width, rows_dev = hidden[0].shape
    shards = len(shard_order)
    group = largest_divisor(slots, 8)
    smem = pl.BlockSpec(memory_space=pltpu.SMEM)
    vmem = pl.BlockSpec(memory_space=pltpu.VMEM)
    hbm = pl.BlockSpec(memory_space=pl.ANY)
    flops = 4 * block_count * slots * tile * tile * width
    return pl.pallas_call(
        functools.partial(tile_kernel, block_count, slots, tile, group, shard_order),
        out_shape=(
            jax.ShapeDtypeStruct((width, rows_dev), BF16),
            jax.ShapeDtypeStruct((shards // 2, width, rows_dev), BF16),
            jax.ShapeDtypeStruct((shards // 2, width, rows_dev), BF16),
        ),
        in_specs=[smem, smem, smem, vmem, vmem, hbm] + [hbm] * shards,
        out_specs=(vmem, vmem, vmem),
        scratch_shapes=[
            pltpu.VMEM(tiles.shape, BF16),
            pltpu.VMEM((shards * block_count, width, tile), BF16),
            pltpu.VMEM((shards * block_count, width, tile), F32),
            pltpu.SemaphoreType.DMA((block_count, slots // group)),
            pltpu.SemaphoreType.DMA((shards, block_count)),
        ],
        compiler_params=pltpu.CompilerParams(vmem_limit_bytes=48 * 1024 * 1024),
        cost_estimate=pl.CostEstimate(
            flops=flops, bytes_accessed=2 * tiles.size, transcendentals=width * rows_dev
        ),
    )(coords.reshape(-1), counts, me.reshape(1), bias[:, None], cotangent, tiles, *hidden)


def sum_dots_kernel(dims, lefts, *refs):
    total = None
    for left, right in zip(refs[:lefts], refs[lefts:-1]):
        term = lax.dot_general(left[...], right[...], (dims, ((), ())), preferred_element_type=F32)
        total = term if total is None else total + term
    refs[-1][...] = total.astype(refs[-1].dtype)


def sum_dots(lefts, rights, dims):
    (left_dim,), (right_dim,) = dims
    out = (lefts[0].shape[1 - left_dim], rights[0].shape[1 - right_dim])
    vmem = pl.BlockSpec(memory_space=pltpu.VMEM)
    depth = sum(v.shape[left_dim] for v in lefts)
    return pl.pallas_call(
        functools.partial(sum_dots_kernel, dims, len(lefts)),
        out_shape=jax.ShapeDtypeStruct(out, BF16),
        in_specs=[vmem] * (2 * len(lefts)),
        out_specs=vmem,
        compiler_params=pltpu.CompilerParams(vmem_limit_bytes=48 * 1024 * 1024),
        cost_estimate=pl.CostEstimate(
            flops=2 * out[0] * out[1] * depth,
            bytes_accessed=2 * depth * (out[0] + out[1]),
            transcendentals=0,
        ),
    )(*lefts, *rights)


def weight_part_kernel(scale, order, col_ref, grad_ref, *refs):
    grad = grad_ref[...]
    out_ref = refs[-1]
    for k, x_ref in zip(order, refs[:-1]):
        width = x_ref.shape[0]
        start = pl.multiple_of((col_ref[0] ^ k) * width, 16)
        part = lax.dot_general(
            x_ref[...], grad, (((1,), (1,)), ((), ())), preferred_element_type=F32
        )
        out_ref[pl.ds(start, width), :] = part * scale


def weight_part(scale, order, col, grad, x_parts):
    width = grad.shape[0]
    vmem = pl.BlockSpec(memory_space=pltpu.VMEM)
    smem = pl.BlockSpec(memory_space=pltpu.SMEM)
    out = (width * len(x_parts), width)
    return pl.pallas_call(
        functools.partial(weight_part_kernel, scale, order),
        out_shape=jax.ShapeDtypeStruct(out, F32),
        in_specs=[smem, vmem] + [vmem] * len(x_parts),
        out_specs=vmem,
        compiler_params=pltpu.CompilerParams(vmem_limit_bytes=48 * 1024 * 1024),
        cost_estimate=pl.CostEstimate(
            flops=2 * out[0] * out[1] * grad.shape[1],
            bytes_accessed=2 * grad.size * (len(x_parts) + 1) + 4 * out[0] * out[1],
            transcendentals=0,
        ),
    )(col.reshape(1), grad, *x_parts)


def swap(value, axis, k):
    return lax.ppermute(value, axis, [(i, i ^ k) for i in range(lax.axis_size(axis))])


def local(features, weight, bias, tile_values, tile_coords, tile_counts, cotangent):
    rows_dev, width = features.shape
    n_rows, n_cols = lax.axis_size("rows"), lax.axis_size("cols")
    me, col = lax.axis_index("rows"), lax.axis_index("cols")
    if not all(n & (n - 1) == 0 for n in (n_rows, n_cols)):
        return local_any(features, weight, bias, tile_values, tile_coords, tile_counts, cotangent)
    cols_order = tuple(range(n_cols))
    chips = tuple(range(0, n_rows, 2))

    x = features.T
    x_parts = [x] + [swap(x, "cols", k) for k in cols_order[1:]]
    weight_down = [
        lax.dynamic_slice(weight, ((col ^ k) * width, col * width), (width, width))
        for k in cols_order
    ]
    weight_across = [
        lax.dynamic_slice(weight, (col * width, (col ^ k) * width), (width, width))
        for k in cols_order
    ]
    hidden = sum_dots(weight_down, x_parts, ((0,), (0,)))

    own = [hidden] + [swap(hidden, "rows", k) for k in chips[1:]]
    other = [swap(h, "rows", 1) for h in own]
    order = tuple(k + c for c in (0, 1) for k in chips)
    act, keep, send = tile_products(
        order, own + other, tile_coords, tile_counts, me, bias, cotangent.T, tile_values
    )
    got = swap(send, "rows", 1)
    chip_sum = [keep[j].astype(F32) + got[j].astype(F32) for j in range(len(chips))]
    total = chip_sum[0]
    for j, k in enumerate(chips[1:], 1):
        total = total + swap(chip_sum[j].astype(BF16), "rows", k).astype(F32)
    grad_hidden = total.astype(BF16)

    scale = 1.0 / math.sqrt(rows_dev * n_rows)
    part = weight_part(scale, cols_order, col, grad_hidden, x_parts)
    part = part.reshape(n_rows, -1, width)
    part_send = jnp.stack([part[me ^ (k + 1)] for k in chips]).astype(BF16)
    part_got = swap(part_send, "rows", 1)
    weight_grad = part[me] + part_got[0].astype(F32)
    for j, k in enumerate(chips[1:], 1):
        both = (part[me ^ k] + part_got[j].astype(F32)).astype(BF16)
        weight_grad = weight_grad + swap(both, "rows", k).astype(F32)

    grads = [grad_hidden] + [swap(grad_hidden, "cols", k) for k in cols_order[1:]]
    input_grad = sum_dots(weight_across, grads, ((1,), (0,)))
    return (act.T, input_grad.T, weight_grad)


def contract_first(a, b):
    return lax.dot_general(a, b, (((0,), (0,)), ((), ())), preferred_element_type=F32)


def local_any(features, weight, bias, tile_values, tile_coords, tile_counts, cotangent):
    rows_dev, col_width = features.shape
    n_rows = lax.axis_size("rows")
    col_start = lax.axis_index("cols") * col_width
    x_full = lax.all_gather(features.T, "cols", axis=0, tiled=True)
    w_cols = lax.dynamic_slice_in_dim(weight, col_start, col_width, 1)
    hidden = contract_first(w_cols, x_full).astype(BF16)
    all_hidden = lax.all_gather(hidden, "rows", axis=0)
    order = tuple(range(n_rows))
    act, keep, send = tile_products(
        order,
        [all_hidden[s] for s in order],
        tile_coords,
        tile_counts,
        jnp.zeros((), jnp.int32),
        bias,
        cotangent.T,
        tile_values,
    )
    part = jnp.concatenate([keep, send], axis=0)
    grad_hidden = lax.psum_scatter(part, "rows", scatter_dimension=0, tiled=False)
    w_rows = lax.dynamic_slice_in_dim(weight, col_start, col_width, 0)
    grad_full = lax.all_gather(grad_hidden, "cols", axis=0, tiled=True)
    input_grad = jnp.dot(w_rows, grad_full, preferred_element_type=F32).astype(BF16)
    scale_factor = 1.0 / math.sqrt(rows_dev * n_rows)
    weight_part_sum = lax.dot_general(
        x_full, grad_hidden, (((1,), (1,)), ((), ())), preferred_element_type=F32
    )
    weight_grad = lax.psum_scatter(
        weight_part_sum * scale_factor, "rows", scatter_dimension=0, tiled=True
    )
    return (act.T, input_grad.T, weight_grad)


def solution(mesh):
    return jax.shard_map(
        local,
        mesh=mesh,
        in_specs=(
            P("rows", "cols"),
            P(),
            P("cols"),
            P("rows", None, None, None),
            P("rows", None),
            P("rows"),
            P("rows", "cols"),
        ),
        out_specs=(P("rows", "cols"), P("rows", "cols"), P("rows", "cols")),
        check_vma=False,
    )
```

```python
import functools
import math

import jax
import jax.numpy as jnp
from jax import lax
from jax.experimental import pallas as pl
from jax.experimental.pallas import tpu as pltpu
from jax.sharding import PartitionSpec as P

F32 = jnp.float32
BF16 = jnp.bfloat16
CHUNK = 16
MIB = 1024 * 1024


def largest_divisor(number, limit):
    return max(d for d in range(1, limit + 1) if number % d == 0)


def tile_kernel(
    slots,
    tile,
    group,
    shard_order,
    gathers,
    scatters,
    coords_ref,
    counts_ref,
    me_ref,
    bias_ref,
    cotangent_ref,
    tiles_ref,
    *rest,
):
    shards, block_count = len(shard_order), sum(gathers)
    hidden_refs, rest = rest[: shards * len(gathers)], rest[shards * len(gathers) :]
    act_ref, *part_refs = rest[:-5]
    tiles, hidden, partial, tile_sems, hidden_sems = rest[-5:]
    groups = slots // group
    me = me_ref[0]
    width = act_ref.shape[0]

    def tile_copy(i, q):
        span = pl.ds(q * group, group)
        return pltpu.make_async_copy(
            tiles_ref.at[i, span], tiles.at[i, span], tile_sems.at[i, q]
        )

    hidden_copies = []
    for s in range(shards):
        owner = me ^ shard_order[s]
        block = 0
        for c, count in enumerate(gathers):
            for b in range(count):
                hidden_copies.append(
                    pltpu.make_async_copy(
                        hidden_refs[c * shards + s].at[:, pl.ds(b * tile, tile)],
                        hidden.at[owner * block_count + block],
                        hidden_sems.at[s, block],
                    )
                )
                block += 1
    for copy in hidden_copies:
        copy.start()
    for i in range(block_count):
        for q in range(groups):

            @pl.when(q * group < counts_ref[i])
            def _():
                tile_copy(i, q).start()

    partial[...] = jnp.zeros_like(partial)
    for copy in hidden_copies:
        copy.wait()

    chunk = largest_divisor(slots, CHUNK)

    def several(i, p):
        parts, places = [], []
        for t in range(chunk):
            k = p * chunk + t
            value = tiles[i, k]
            if t:
                value = jnp.where(k < counts_ref[i], value, jnp.zeros_like(value))
            parts.append(value)
            places.append(coords_ref[i * slots + k])
        return jnp.concatenate(parts, axis=1), places

    for i in range(block_count):
        for q in range(groups):

            @pl.when(q * group < counts_ref[i])
            def _():
                tile_copy(i, q).wait()

        steps = (counts_ref[i] + (chunk - 1)) // chunk
        lanes = pl.ds(i * tile, tile)

        def forward(p, total):
            values, places = several(i, p)
            panel = jnp.concatenate([hidden[c] for c in places], axis=1)
            return total + lax.dot_general(
                panel, values, (((1,), (1,)), ((), ())), preferred_element_type=F32
            )

        total = lax.fori_loop(0, steps, forward, jnp.zeros((width, tile), F32))
        pre = total + bias_ref[...]
        s = jax.nn.sigmoid(pre)
        act_ref[:, lanes] = (pre * s).astype(BF16)
        slope = s * (1.0 + pre * (1.0 - s))
        grad = (cotangent_ref[:, lanes].astype(F32) * slope).astype(BF16)

        def backward(p, carry):
            values, places = several(i, p)
            out = jnp.dot(grad, values, preferred_element_type=F32)
            for t, c in enumerate(places):
                partial[c] += out[:, t * tile : (t + 1) * tile]
            return carry

        lax.fori_loop(0, steps, backward, 0)

    half = shards // 2
    first = 0
    for c, count in enumerate(scatters):
        keep_own, keep, send_own, send = part_refs[4 * c : 4 * c + 4]
        for s in range(shards):
            own, others = (keep_own, keep) if s < half else (send_own, send)
            out_ref = own if s % half == 0 else others.at[s % half - 1]
            owner = me ^ shard_order[s]
            for b in range(count):
                value = partial[owner * block_count + first + b].astype(BF16)
                out_ref[:, b * tile : (b + 1) * tile] = value
        first += count


def tile_products(
    shard_order, gathers, scatters, hidden, coords, counts, me, bias, cotangent, tiles
):
    block_count, slots, tile, unused_side = tiles.shape
    width, rows_dev = cotangent.shape
    shards = len(shard_order)
    group = largest_divisor(slots, 8)
    smem = pl.BlockSpec(memory_space=pltpu.SMEM)
    vmem = pl.BlockSpec(memory_space=pltpu.VMEM)
    hbm = pl.BlockSpec(memory_space=pltpu.HBM)
    vmem_bytes = 2 * tiles.size + (6 + 2) * shards * width * rows_dev + 16 * cotangent.size
    flops = 4 * block_count * slots * tile * tile * width
    parts = []
    for count in scatters:
        own = jax.ShapeDtypeStruct((width, count * tile), BF16)
        others = jax.ShapeDtypeStruct((max(shards // 2 - 1, 1), width, count * tile), BF16)
        parts += [own, others] * 2
    flat = [v for chunk in hidden for v in chunk]
    return pl.pallas_call(
        functools.partial(tile_kernel, slots, tile, group, shard_order, gathers, scatters),
        out_shape=(jax.ShapeDtypeStruct((width, rows_dev), BF16), *parts),
        in_specs=[smem, smem, smem, vmem, vmem, hbm] + [hbm] * len(flat),
        out_specs=(vmem,) * (1 + len(parts)),
        scratch_shapes=[
            pltpu.VMEM(tiles.shape, BF16),
            pltpu.VMEM((shards * block_count, width, tile), BF16),
            pltpu.VMEM((shards * block_count, width, tile), F32),
            pltpu.SemaphoreType.DMA((block_count, slots // group)),
            pltpu.SemaphoreType.DMA((shards, block_count)),
        ],
        compiler_params=pltpu.CompilerParams(vmem_limit_bytes=vmem_bytes + MIB),
        cost_estimate=pl.CostEstimate(
            flops=flops, bytes_accessed=2 * tiles.size, transcendentals=width * rows_dev
        ),
    )(
        coords.reshape(-1),
        counts,
        me.reshape(1),
        bias[:, None],
        cotangent,
        *[in_hbm(v) for v in (tiles, *flat)],
    )


def in_vmem(value):
    return pltpu.with_memory_space_constraint(value, pltpu.VMEM)


def in_hbm(value):
    return pltpu.with_memory_space_constraint(value, pltpu.HBM)


VMEM = pl.BlockSpec(memory_space=pltpu.VMEM)
ANY = pl.BlockSpec(memory_space=pl.ANY)


def small_call(kernel, out_shape, values, after, pinned=True):
    outs = jax.tree.leaves(out_shape)
    touched = sum(v.size * v.dtype.itemsize for v in (*values, *outs))
    return pl.pallas_call(
        kernel,
        out_shape=out_shape,
        in_specs=[VMEM] * len(values) + [ANY] * len(after),
        out_specs=jax.tree.map(lambda _: VMEM, out_shape),
        compiler_params=pltpu.CompilerParams(vmem_limit_bytes=2 * touched + 2 * MIB),
        cost_estimate=pl.CostEstimate(flops=0, bytes_accessed=0, transcendentals=0),
    )(*[in_vmem(v) for v in values] if pinned else values, *after)


def sum_dots(lefts, rights, dims, before=(), after=()):
    (left_dim,), unused_right = dims
    number = len(lefts)
    rows, cols = lefts[0].shape[1 - left_dim], rights[0].shape[1]
    skip = sum(v.shape[1] for v in before)

    def kernel(*refs):
        total = None
        for left, right in zip(refs[:number], refs[number : 2 * number]):
            term = lax.dot_general(
                left[...], right[...], (dims, ((), ())), preferred_element_type=F32
            )
            total = term if total is None else total + term
        start = 0
        for ref in refs[2 * number : 2 * number + len(before)]:
            refs[-1][:, start : start + ref.shape[1]] = ref[...]
            start += ref.shape[1]
        refs[-1][:, skip:] = total.astype(BF16)

    out = jax.ShapeDtypeStruct((rows, skip + cols), BF16)
    return small_call(kernel, out, (*lefts, *rights, *before), after, False)


def add_up(values, dtype, after=()):
    number = len(values)

    def kernel(*refs):
        total = refs[0][...].astype(F32)
        for ref in refs[1:number]:
            total = total + ref[...].astype(F32)
        refs[-1][...] = total.astype(dtype)

    out = jax.ShapeDtypeStruct(values[0].shape, dtype)
    return small_call(kernel, out, values, after)


def chip_sums(keep, got, after=()):
    number = keep.shape[0]

    def kernel(keep_ref, got_ref, *refs):
        for j, out_ref in enumerate(refs[len(after) :]):
            out_ref[...] = (keep_ref[j].astype(F32) + got_ref[j].astype(F32)).astype(BF16)

    out = (jax.ShapeDtypeStruct(keep.shape[1:], BF16),) * number
    return small_call(kernel, out, (keep, got), after)


def weight_parts(scale, cols_order, rows_order, col, me, grads, x_parts, after=()):
    width = grads[0].shape[0]
    rows_dev = sum(g.shape[1] for g in grads)
    n_rows = len(rows_order)
    half = n_rows // 2
    rows_out = width * len(cols_order) // n_rows
    pieces = len(x_parts[0])
    values = (*grads, *[p for parts in x_parts for p in parts])

    def kernel(col_ref, me_ref, *refs):
        inputs = refs[: len(values)]
        own_ref, keep_ref, send_own_ref, send_ref, grad, xs, part, sems = refs[-8:]
        copies = []

        def fill(target, sources, first_sem):
            start = 0
            for j, source in enumerate(sources):
                lanes = pl.ds(start, source.shape[1])
                copy = pltpu.make_async_copy(source, target.at[:, lanes], sems.at[first_sem + j])
                copy.start()
                copies.append(copy)
                start += source.shape[1]

        fill(grad, inputs[: len(grads)], 0)
        for j in range(len(cols_order)):
            first = len(grads) + j * pieces
            fill(xs.at[j], inputs[first : first + pieces], first)
        for copy in copies:
            copy.wait()
        for j, k in enumerate(cols_order):
            start = pl.multiple_of((col_ref[0] ^ k) * width, 16)
            product = lax.dot_general(
                xs[j], grad[...], (((1,), (1,)), ((), ())), preferred_element_type=F32
            )
            part[pl.ds(start, width), :] = product * scale
        for j, k in enumerate(rows_order):
            start = pl.multiple_of((me_ref[0] ^ k) * rows_out, 8)
            value = part[pl.ds(start, rows_out), :]
            if j == 0:
                own_ref[...] = value
            elif j < half:
                keep_ref[j - 1] = value
            elif j == half:
                send_own_ref[...] = value.astype(BF16)
            else:
                send_ref[j - half - 1] = value.astype(BF16)

    touched = 2 * width * rows_dev * (len(cols_order) + 1) + 8 * width * width * len(cols_order)
    smem = pl.BlockSpec(memory_space=pltpu.SMEM)
    others = max(half - 1, 1)
    return pl.pallas_call(
        kernel,
        out_shape=(
            jax.ShapeDtypeStruct((rows_out, width), F32),
            jax.ShapeDtypeStruct((others, rows_out, width), F32),
            jax.ShapeDtypeStruct((rows_out, width), BF16),
            jax.ShapeDtypeStruct((others, rows_out, width), BF16),
        ),
        in_specs=[smem, smem] + [ANY] * (len(values) + len(after)),
        out_specs=(VMEM,) * 4,
        scratch_shapes=[
            pltpu.VMEM((width, rows_dev), BF16),
            pltpu.VMEM((len(cols_order), width, rows_dev), BF16),
            pltpu.VMEM((width * len(cols_order), width), F32),
            pltpu.SemaphoreType.DMA((len(values),)),
        ],
        compiler_params=pltpu.CompilerParams(vmem_limit_bytes=2 * touched + 2 * MIB),
        cost_estimate=pl.CostEstimate(flops=0, bytes_accessed=0, transcendentals=0),
    )(col.reshape(1), me.reshape(1), *values, *after)


def swap(value, axis, k):
    return lax.ppermute(value, axis, [(i, i ^ k) for i in range(lax.axis_size(axis))])


def local(features, weight, bias, tile_values, tile_coords, tile_counts, cotangent):
    rows_dev, width = features.shape
    n_rows, n_cols = lax.axis_size("rows"), lax.axis_size("cols")
    me, col = lax.axis_index("rows"), lax.axis_index("cols")
    simple = all(n > 1 and n & (n - 1) == 0 for n in (n_rows, n_cols)) and n_rows > 2
    if not simple or width * n_cols % (8 * n_rows) or width % 16:
        return local_any(features, weight, bias, tile_values, tile_coords, tile_counts, cotangent)
    cols_order = tuple(range(n_cols))
    chips = tuple(range(0, n_rows, 2))
    block_count, unused_slots, tile, unused_side = tile_values.shape
    small = block_count // 2
    gathers = (block_count - small, small) if small else (block_count,)
    scatters = gathers[::-1]

    x = features.T
    x_parts, start = [], 0
    for count in gathers:
        piece = x[:, start * tile : (start + count) * tile]
        x_parts.append([piece] + [swap(piece, "cols", k) for k in cols_order[1:]])
        start += count
    weight_down = [
        lax.dynamic_slice(weight, ((col ^ k) * width, col * width), (width, width))
        for k in cols_order
    ]
    weight_across = [
        lax.dynamic_slice(weight, (col * width, (col ^ k) * width), (width, width))
        for k in cols_order
    ]

    order = tuple(k + c for c in (0, 1) for k in chips)
    shards = []
    for parts in x_parts:
        hidden = sum_dots(weight_down, parts, ((0,), (0,)))
        own = [hidden] + [swap(hidden, "rows", k) for k in chips[1:]]
        shards.append(own + [swap(part, "rows", 1) for part in own])

    act, *part = tile_products(
        order,
        gathers,
        scatters,
        shards,
        tile_coords,
        tile_counts,
        me,
        bias,
        cotangent.T,
        tile_values,
    )

    grads, arrived, input_grad = [], (), ()
    for c in range(len(scatters)):
        keep_own, keep, send_own, send = part[4 * c : 4 * c + 4]
        got, got_own = swap(send, "rows", 1), swap(send_own, "rows", 1)
        sums = chip_sums(keep, got, arrived)
        arrived = tuple(swap(v, "rows", k) for v, k in zip(sums, chips[1:]))
        grad = add_up((keep_own, got_own, *arrived), BF16)
        grads.append([grad] + [swap(grad, "cols", k) for k in cols_order[1:]])

    own, keep, send_own, send = weight_parts(
        1.0 / math.sqrt(rows_dev * n_rows),
        cols_order,
        order,
        col,
        me,
        [g[0] for g in grads],
        list(zip(*x_parts)),
        tuple(grads[0][1:]) if len(grads) > 1 else (),
    )
    got, got_own = swap(send, "rows", 1), swap(send_own, "rows", 1)
    weight_grad = add_up(
        (own, got_own, *[swap(v, "rows", k) for v, k in zip(chip_sums(keep, got), chips[1:])]), F32
    )

    for c, values in enumerate(grads):
        last = (weight_grad,) if c + 1 == len(grads) else ()
        input_grad = (sum_dots(weight_across, values, ((1,), (0,)), input_grad, last),)
    return (act.T, input_grad[0].T, weight_grad)


def contract_first(a, b):
    return lax.dot_general(a, b, (((0,), (0,)), ((), ())), preferred_element_type=F32)


def local_any(features, weight, bias, tile_values, tile_coords, tile_counts, cotangent):
    rows_dev, col_width = features.shape
    n_rows = lax.axis_size("rows")
    col_start = lax.axis_index("cols") * col_width
    x_full = lax.all_gather(features.T, "cols", axis=0, tiled=True)
    w_cols = lax.dynamic_slice_in_dim(weight, col_start, col_width, 1)
    hidden = contract_first(w_cols, x_full).astype(BF16)
    all_hidden = lax.all_gather(hidden, "rows", axis=0)
    order = tuple(range(n_rows))
    act, keep_own, keep, send_own, send = tile_products(
        order,
        (tile_values.shape[0],),
        (tile_values.shape[0],),
        [[all_hidden[s] for s in order]],
        tile_coords,
        tile_counts,
        jnp.zeros((), jnp.int32),
        bias,
        cotangent.T,
        tile_values,
    )
    part = jnp.concatenate([keep_own[None], keep, send_own[None], send], axis=0)
    grad_hidden = lax.psum_scatter(part, "rows", scatter_dimension=0, tiled=False)
    w_rows = lax.dynamic_slice_in_dim(weight, col_start, col_width, 0)
    grad_full = lax.all_gather(grad_hidden, "cols", axis=0, tiled=True)
    input_grad = jnp.dot(w_rows, grad_full, preferred_element_type=F32).astype(BF16)
    scale_factor = 1.0 / math.sqrt(rows_dev * n_rows)
    weight_part_sum = lax.dot_general(
        x_full, grad_hidden, (((1,), (1,)), ((), ())), preferred_element_type=F32
    )
    weight_grad = lax.psum_scatter(
        weight_part_sum * scale_factor, "rows", scatter_dimension=0, tiled=True
    )
    return (act.T, input_grad.T, weight_grad)


def solution(mesh):
    return jax.shard_map(
        local,
        mesh=mesh,
        in_specs=(
            P("rows", "cols"),
            P(),
            P("cols"),
            P("rows", None, None, None),
            P("rows", None),
            P("rows"),
            P("rows", "cols"),
        ),
        out_specs=(P("rows", "cols"), P("rows", "cols"), P("rows", "cols")),
        check_vma=False,
    )
```

```python
import functools
import math

import jax
import jax.numpy as jnp
from jax import lax
from jax.experimental import pallas as pl
from jax.experimental.pallas import tpu as pltpu
from jax.sharding import PartitionSpec as P

F32 = jnp.float32
BF16 = jnp.bfloat16
CHUNK = 16
MIB = 1024 * 1024


def largest_divisor(number, limit):
    return max(d for d in range(1, limit + 1) if number % d == 0)


def tile_kernel(
    slots,
    tile,
    group,
    shard_order,
    gathers,
    scatters,
    places,
    inputs,
    coords_ref,
    counts_ref,
    me_ref,
    bias_ref,
    cotangent_ref,
    tiles_ref,
    *rest,
):
    shards, block_count = len(shard_order), sum(gathers)
    hidden_refs, act_ref, part_refs = rest[:inputs], rest[inputs], rest[inputs + 1 : -5]
    tiles, hidden, partial, tile_sems, hidden_sems = rest[-5:]
    groups = slots // group
    me = me_ref[0]
    width = act_ref.shape[0]

    def tile_copy(i, q):
        span = pl.ds(q * group, group)
        return pltpu.make_async_copy(
            tiles_ref.at[i, span], tiles.at[i, span], tile_sems.at[i, q]
        )

    def source(c, s):
        place, entry = places[c][s]
        return hidden_refs[place] if entry is None else hidden_refs[place].at[entry]

    hidden_copies = []
    for s in range(shards):
        owner = me ^ shard_order[s]
        block = 0
        for c, count in enumerate(gathers):
            for b in range(count):
                hidden_copies.append(
                    pltpu.make_async_copy(
                        source(c, s).at[:, pl.ds(b * tile, tile)],
                        hidden.at[owner * block_count + block],
                        hidden_sems.at[s, block],
                    )
                )
                block += 1
    for copy in hidden_copies:
        copy.start()
    for i in range(block_count):
        for q in range(groups):

            @pl.when(q * group < counts_ref[i])
            def _():
                tile_copy(i, q).start()

    partial[...] = jnp.zeros_like(partial)
    for copy in hidden_copies:
        copy.wait()

    chunk = largest_divisor(slots, CHUNK)

    def several(i, p):
        parts, places = [], []
        for t in range(chunk):
            k = p * chunk + t
            value = tiles[i, k]
            if t:
                value = jnp.where(k < counts_ref[i], value, jnp.zeros_like(value))
            parts.append(value)
            places.append(coords_ref[i * slots + k])
        return jnp.concatenate(parts, axis=1), places

    for i in range(block_count):
        for q in range(groups):

            @pl.when(q * group < counts_ref[i])
            def _():
                tile_copy(i, q).wait()

        steps = (counts_ref[i] + (chunk - 1)) // chunk
        lanes = pl.ds(i * tile, tile)

        def forward(p, total):
            values, places = several(i, p)
            panel = jnp.concatenate([hidden[c] for c in places], axis=1)
            return total + lax.dot_general(
                panel, values, (((1,), (1,)), ((), ())), preferred_element_type=F32
            )

        total = lax.fori_loop(0, steps, forward, jnp.zeros((width, tile), F32))
        pre = total + bias_ref[...]
        s = jax.nn.sigmoid(pre)
        act_ref[:, lanes] = (pre * s).astype(BF16)
        slope = s * (1.0 + pre * (1.0 - s))
        grad = (cotangent_ref[:, lanes].astype(F32) * slope).astype(BF16)

        def backward(p, carry):
            values, places = several(i, p)
            out = jnp.dot(grad, values, preferred_element_type=F32)
            for t, c in enumerate(places):
                partial[c] += out[:, t * tile : (t + 1) * tile]
            return carry

        lax.fori_loop(0, steps, backward, 0)

    half = shards // 2
    first = 0
    for c, count in enumerate(scatters):
        for s in range(shards):
            out_ref = part_refs[2 * c + s // half].at[s % half]
            owner = me ^ shard_order[s]
            for b in range(count):
                value = partial[owner * block_count + first + b].astype(BF16)
                out_ref[:, b * tile : (b + 1) * tile] = value
        first += count


def tile_products(
    shard_order, gathers, scatters, hidden, coords, counts, me, bias, cotangent, tiles
):
    block_count, slots, tile, unused_side = tiles.shape
    width, rows_dev = cotangent.shape
    shards = len(shard_order)
    group = largest_divisor(slots, 8)
    smem = pl.BlockSpec(memory_space=pltpu.SMEM)
    vmem = pl.BlockSpec(memory_space=pltpu.VMEM)
    hbm = pl.BlockSpec(memory_space=pltpu.HBM)
    vmem_bytes = 2 * tiles.size + (6 + 2) * shards * width * rows_dev + 16 * cotangent.size
    flops = 4 * block_count * slots * tile * tile * width
    parts = []
    for count in scatters:
        parts += [jax.ShapeDtypeStruct((shards // 2, width, count * tile), BF16)] * 2
    flat, places = [], []
    for chunk in hidden:
        entries = []
        for value in chunk:
            inner = [None] if value.ndim == 2 else range(value.shape[0])
            entries += [(len(flat), entry) for entry in inner]
            flat.append(value)
        places.append(entries)
    return pl.pallas_call(
        functools.partial(
            tile_kernel, slots, tile, group, shard_order, gathers, scatters, places, len(flat)
        ),
        out_shape=(jax.ShapeDtypeStruct((width, rows_dev), BF16), *parts),
        in_specs=[smem, smem, smem, vmem, vmem, hbm] + [hbm] * len(flat),
        out_specs=(vmem,) * (1 + len(parts)),
        scratch_shapes=[
            pltpu.VMEM(tiles.shape, BF16),
            pltpu.VMEM((shards * block_count, width, tile), BF16),
            pltpu.VMEM((shards * block_count, width, tile), F32),
            pltpu.SemaphoreType.DMA((block_count, slots // group)),
            pltpu.SemaphoreType.DMA((shards, block_count)),
        ],
        compiler_params=pltpu.CompilerParams(vmem_limit_bytes=vmem_bytes + MIB),
        cost_estimate=pl.CostEstimate(
            flops=flops, bytes_accessed=2 * tiles.size, transcendentals=width * rows_dev
        ),
    )(
        coords.reshape(-1),
        counts,
        me.reshape(1),
        bias[:, None],
        cotangent,
        *[in_hbm(v) for v in (tiles, *flat)],
    )


def in_vmem(value):
    return pltpu.with_memory_space_constraint(value, pltpu.VMEM)


def in_hbm(value):
    return pltpu.with_memory_space_constraint(value, pltpu.HBM)


VMEM = pl.BlockSpec(memory_space=pltpu.VMEM)
ANY = pl.BlockSpec(memory_space=pl.ANY)


def small_call(kernel, out_shape, values, after, pinned=True):
    outs = jax.tree.leaves(out_shape)
    touched = sum(v.size * v.dtype.itemsize for v in (*values, *outs))
    return pl.pallas_call(
        kernel,
        out_shape=out_shape,
        in_specs=[VMEM] * len(values) + [ANY] * len(after),
        out_specs=jax.tree.map(lambda _: VMEM, out_shape),
        compiler_params=pltpu.CompilerParams(vmem_limit_bytes=2 * touched + 2 * MIB),
        cost_estimate=pl.CostEstimate(flops=0, bytes_accessed=0, transcendentals=0),
    )(*[in_vmem(v) for v in values] if pinned else values, *after)


def sum_dots(lefts, rights, dims, before=(), after=()):
    (left_dim,), unused_right = dims
    number = len(lefts)
    rows, cols = lefts[0].shape[1 - left_dim], rights[0].shape[1]
    skip = sum(v.shape[1] for v in before)

    def kernel(*refs):
        total = None
        for left, right in zip(refs[:number], refs[number : 2 * number]):
            term = lax.dot_general(
                left[...], right[...], (dims, ((), ())), preferred_element_type=F32
            )
            total = term if total is None else total + term
        start = 0
        for ref in refs[2 * number : 2 * number + len(before)]:
            refs[-1][:, start : start + ref.shape[1]] = ref[...]
            start += ref.shape[1]
        refs[-1][:, skip:] = total.astype(BF16)

    out = jax.ShapeDtypeStruct((rows, skip + cols), BF16)
    return small_call(kernel, out, (*lefts, *rights, *before), after, False)


def pack(values):
    out = jax.ShapeDtypeStruct((len(values),) + values[0].shape, values[0].dtype)

    def kernel(*refs):
        for j, ref in enumerate(refs[:-1]):
            refs[-1][j] = ref[...]

    return small_call(kernel, out, values, (), False)


def add_up(values, dtype, after=()):
    number = len(values)

    def kernel(*refs):
        total = None
        for ref in refs[:number]:
            value = (ref[0] if len(ref.shape) == 3 else ref[...]).astype(F32)
            total = value if total is None else total + value
        refs[-1][...] = total.astype(dtype)

    out = jax.ShapeDtypeStruct(values[0].shape[-2:], dtype)
    return small_call(kernel, out, values, after)


def chip_sums(keep, got, after=()):
    number = keep.shape[0] - 1

    def kernel(keep_ref, got_ref, *refs):
        for j, out_ref in enumerate(refs[len(after) :], 1):
            out_ref[...] = (keep_ref[j].astype(F32) + got_ref[j].astype(F32)).astype(BF16)

    out = (jax.ShapeDtypeStruct(keep.shape[1:], BF16),) * number
    return small_call(kernel, out, (keep, got), after)


def weight_parts(scale, cols_order, rows_order, col, me, grads, x_parts, after=()):
    width = grads[0].shape[0]
    rows_dev = sum(g.shape[1] for g in grads)
    n_rows = len(rows_order)
    half = n_rows // 2
    rows_out = width * len(cols_order) // n_rows
    pieces = len(x_parts[0])
    values = (*grads, *[p for parts in x_parts for p in parts])

    def kernel(col_ref, me_ref, *refs):
        inputs = refs[: len(values)]
        keep_ref, send_ref, grad, xs, part, sems = refs[-6:]
        copies = []

        def fill(target, sources, first_sem):
            start = 0
            for j, source in enumerate(sources):
                lanes = pl.ds(start, source.shape[1])
                copy = pltpu.make_async_copy(source, target.at[:, lanes], sems.at[first_sem + j])
                copy.start()
                copies.append(copy)
                start += source.shape[1]

        fill(grad, inputs[: len(grads)], 0)
        for j in range(len(cols_order)):
            first = len(grads) + j * pieces
            fill(xs.at[j], inputs[first : first + pieces], first)
        for copy in copies:
            copy.wait()
        for j, k in enumerate(cols_order):
            start = pl.multiple_of((col_ref[0] ^ k) * width, 16)
            product = lax.dot_general(
                xs[j], grad[...], (((1,), (1,)), ((), ())), preferred_element_type=F32
            )
            part[pl.ds(start, width), :] = product * scale
        for j, k in enumerate(rows_order):
            start = pl.multiple_of((me_ref[0] ^ k) * rows_out, 8)
            value = part[pl.ds(start, rows_out), :]
            if j < half:
                keep_ref[j] = value
            else:
                send_ref[j - half] = value.astype(BF16)

    touched = 2 * width * rows_dev * (len(cols_order) + 1) + 8 * width * width * len(cols_order)
    smem = pl.BlockSpec(memory_space=pltpu.SMEM)
    return pl.pallas_call(
        kernel,
        out_shape=(
            jax.ShapeDtypeStruct((half, rows_out, width), F32),
            jax.ShapeDtypeStruct((half, rows_out, width), BF16),
        ),
        in_specs=[smem, smem] + [ANY] * (len(values) + len(after)),
        out_specs=(VMEM,) * 2,
        scratch_shapes=[
            pltpu.VMEM((width, rows_dev), BF16),
            pltpu.VMEM((len(cols_order), width, rows_dev), BF16),
            pltpu.VMEM((width * len(cols_order), width), F32),
            pltpu.SemaphoreType.DMA((len(values),)),
        ],
        compiler_params=pltpu.CompilerParams(vmem_limit_bytes=2 * touched + 2 * MIB),
        cost_estimate=pl.CostEstimate(flops=0, bytes_accessed=0, transcendentals=0),
    )(col.reshape(1), me.reshape(1), *values, *after)


def swap(value, axis, k):
    return lax.ppermute(value, axis, [(i, i ^ k) for i in range(lax.axis_size(axis))])


def local(features, weight, bias, tile_values, tile_coords, tile_counts, cotangent):
    rows_dev, width = features.shape
    n_rows, n_cols = lax.axis_size("rows"), lax.axis_size("cols")
    me, col = lax.axis_index("rows"), lax.axis_index("cols")
    simple = all(n > 1 and n & (n - 1) == 0 for n in (n_rows, n_cols)) and n_rows > 2
    if not simple or width * n_cols % (8 * n_rows) or width % 16:
        return local_any(features, weight, bias, tile_values, tile_coords, tile_counts, cotangent)
    cols_order = tuple(range(n_cols))
    chips = tuple(range(0, n_rows, 2))
    block_count, unused_slots, tile, unused_side = tile_values.shape
    small = block_count // 2
    gathers = (block_count - small, small) if small else (block_count,)
    scatters = gathers[::-1]

    x = features.T
    x_parts, start = [], 0
    for count in gathers:
        piece = x[:, start * tile : (start + count) * tile]
        x_parts.append([piece] + [swap(piece, "cols", k) for k in cols_order[1:]])
        start += count
    weight_down = [
        lax.dynamic_slice(weight, ((col ^ k) * width, col * width), (width, width))
        for k in cols_order
    ]
    weight_across = [
        lax.dynamic_slice(weight, (col * width, (col ^ k) * width), (width, width))
        for k in cols_order
    ]

    order = tuple(k + c for c in (0, 1) for k in chips)
    shards = []
    for parts in x_parts:
        hidden = sum_dots(weight_down, parts, ((0,), (0,)))
        own = [hidden] + [swap(hidden, "rows", k) for k in chips[1:]]
        shards.append(own + [swap(part, "rows", 1) for part in own])

    act, *part = tile_products(
        order,
        gathers,
        scatters,
        shards,
        tile_coords,
        tile_counts,
        me,
        bias,
        cotangent.T,
        tile_values,
    )

    grads, arrived, input_grad = [], (), ()
    for c in range(len(scatters)):
        keep, send = part[2 * c : 2 * c + 2]
        got = swap(send, "rows", 1)
        sums = chip_sums(keep, got, arrived)
        arrived = tuple(swap(v, "rows", k) for v, k in zip(sums, chips[1:]))
        grad = add_up((keep, got, *arrived), BF16)
        grads.append([grad] + [swap(grad, "cols", k) for k in cols_order[1:]])

    keep, send = weight_parts(
        1.0 / math.sqrt(rows_dev * n_rows),
        cols_order,
        order,
        col,
        me,
        [g[0] for g in grads],
        list(zip(*x_parts)),
        tuple(grads[0][1:]) if len(grads) > 1 else (),
    )
    got = swap(send, "rows", 1)
    sums = chip_sums(keep, got)
    weight_grad = add_up((keep, got, *[swap(v, "rows", k) for v, k in zip(sums, chips[1:])]), F32)

    for c, values in enumerate(grads):
        last = (weight_grad,) if c + 1 == len(grads) else ()
        input_grad = (sum_dots(weight_across, values, ((1,), (0,)), input_grad, last),)
    return (act.T, input_grad[0].T, weight_grad)


def contract_first(a, b):
    return lax.dot_general(a, b, (((0,), (0,)), ((), ())), preferred_element_type=F32)


def local_any(features, weight, bias, tile_values, tile_coords, tile_counts, cotangent):
    rows_dev, col_width = features.shape
    n_rows = lax.axis_size("rows")
    col_start = lax.axis_index("cols") * col_width
    x_full = lax.all_gather(features.T, "cols", axis=0, tiled=True)
    w_cols = lax.dynamic_slice_in_dim(weight, col_start, col_width, 1)
    hidden = contract_first(w_cols, x_full).astype(BF16)
    all_hidden = lax.all_gather(hidden, "rows", axis=0)
    order = tuple(range(n_rows))
    act, keep, send = tile_products(
        order,
        (tile_values.shape[0],),
        (tile_values.shape[0],),
        [[all_hidden[s] for s in order]],
        tile_coords,
        tile_counts,
        jnp.zeros((), jnp.int32),
        bias,
        cotangent.T,
        tile_values,
    )
    part = jnp.concatenate([keep, send], axis=0)
    grad_hidden = lax.psum_scatter(part, "rows", scatter_dimension=0, tiled=False)
    w_rows = lax.dynamic_slice_in_dim(weight, col_start, col_width, 0)
    grad_full = lax.all_gather(grad_hidden, "cols", axis=0, tiled=True)
    input_grad = jnp.dot(w_rows, grad_full, preferred_element_type=F32).astype(BF16)
    scale_factor = 1.0 / math.sqrt(rows_dev * n_rows)
    weight_part_sum = lax.dot_general(
        x_full, grad_hidden, (((1,), (1,)), ((), ())), preferred_element_type=F32
    )
    weight_grad = lax.psum_scatter(
        weight_part_sum * scale_factor, "rows", scatter_dimension=0, tiled=True
    )
    return (act.T, input_grad.T, weight_grad)


def solution(mesh):
    return jax.shard_map(
        local,
        mesh=mesh,
        in_specs=(
            P("rows", "cols"),
            P(),
            P("cols"),
            P("rows", None, None, None),
            P("rows", None),
            P("rows"),
            P("rows", "cols"),
        ),
        out_specs=(P("rows", "cols"), P("rows", "cols"), P("rows", "cols")),
        check_vma=False,
    )
```

```python
import functools
import math

import jax
import jax.numpy as jnp
from jax import lax
from jax.experimental import pallas as pl
from jax.experimental.pallas import tpu as pltpu
from jax.sharding import PartitionSpec as P

F32 = jnp.float32
BF16 = jnp.bfloat16
CHUNK = 16
MIB = 1024 * 1024


def largest_divisor(number, limit):
    return max(d for d in range(1, limit + 1) if number % d == 0)


def tile_kernel(
    slots,
    tile,
    group,
    shard_order,
    gathers,
    scatters,
    places,
    inputs,
    coords_ref,
    counts_ref,
    me_ref,
    bias_ref,
    cotangent_ref,
    tiles_ref,
    *rest,
):
    shards, block_count = len(shard_order), sum(gathers)
    hidden_refs, act_ref, part_refs = rest[:inputs], rest[inputs], rest[inputs + 1 : -5]
    tiles, hidden, partial, tile_sems, hidden_sems = rest[-5:]
    groups = slots // group
    me = me_ref[0]
    width = act_ref.shape[0]

    def tile_copy(i, q):
        span = pl.ds(q * group, group)
        return pltpu.make_async_copy(
            tiles_ref.at[i, span], tiles.at[i, span], tile_sems.at[i, q]
        )

    def source(c, s):
        place, entry = places[c][s]
        return hidden_refs[place] if entry is None else hidden_refs[place].at[entry]

    hidden_copies = []
    for s in range(shards):
        owner = me ^ shard_order[s]
        block = 0
        for c, count in enumerate(gathers):
            for b in range(count):
                hidden_copies.append(
                    pltpu.make_async_copy(
                        source(c, s).at[:, pl.ds(b * tile, tile)],
                        hidden.at[owner * block_count + block],
                        hidden_sems.at[s, block],
                    )
                )
                block += 1
    for copy in hidden_copies:
        copy.start()
    for i in range(block_count):
        for q in range(groups):

            @pl.when(q * group < counts_ref[i])
            def _():
                tile_copy(i, q).start()

    partial[...] = jnp.zeros_like(partial)
    for copy in hidden_copies:
        copy.wait()

    chunk = largest_divisor(slots, CHUNK)

    def several(i, p):
        parts, places = [], []
        for t in range(chunk):
            k = p * chunk + t
            value = tiles[i, k]
            if t:
                value = jnp.where(k < counts_ref[i], value, jnp.zeros_like(value))
            parts.append(value)
            places.append(coords_ref[i * slots + k])
        return jnp.concatenate(parts, axis=1), places

    for i in range(block_count):
        for q in range(groups):

            @pl.when(q * group < counts_ref[i])
            def _():
                tile_copy(i, q).wait()

        steps = (counts_ref[i] + (chunk - 1)) // chunk
        lanes = pl.ds(i * tile, tile)

        def forward(p, total):
            values, places = several(i, p)
            panel = jnp.concatenate([hidden[c] for c in places], axis=1)
            return total + lax.dot_general(
                panel, values, (((1,), (1,)), ((), ())), preferred_element_type=F32
            )

        total = lax.fori_loop(0, steps, forward, jnp.zeros((width, tile), F32))
        pre = total + bias_ref[...]
        s = jax.nn.sigmoid(pre)
        act_ref[:, lanes] = (pre * s).astype(BF16)
        slope = s * (1.0 + pre * (1.0 - s))
        grad = (cotangent_ref[:, lanes].astype(F32) * slope).astype(BF16)

        def backward(p, carry):
            values, places = several(i, p)
            out = jnp.dot(grad, values, preferred_element_type=F32)
            for t, c in enumerate(places):
                partial[c] += out[:, t * tile : (t + 1) * tile]
            return carry

        lax.fori_loop(0, steps, backward, 0)

    half = shards // 2
    first = 0
    for c, count in enumerate(scatters):
        for s in range(shards):
            out_ref = part_refs[2 * c + s // half].at[s % half]
            owner = me ^ shard_order[s]
            for b in range(count):
                value = partial[owner * block_count + first + b].astype(BF16)
                out_ref[:, b * tile : (b + 1) * tile] = value
        first += count


def tile_products(
    shard_order, gathers, scatters, hidden, coords, counts, me, bias, cotangent, tiles
):
    block_count, slots, tile, unused_side = tiles.shape
    width, rows_dev = cotangent.shape
    shards = len(shard_order)
    group = largest_divisor(slots, 8)
    smem = pl.BlockSpec(memory_space=pltpu.SMEM)
    vmem = pl.BlockSpec(memory_space=pltpu.VMEM)
    hbm = pl.BlockSpec(memory_space=pltpu.HBM)
    vmem_bytes = 2 * tiles.size + (6 + 2) * shards * width * rows_dev + 16 * cotangent.size
    flops = 4 * block_count * slots * tile * tile * width
    parts = []
    for count in scatters:
        parts += [jax.ShapeDtypeStruct((shards // 2, width, count * tile), BF16)] * 2
    flat, places = [], []
    for chunk in hidden:
        entries = []
        for value in chunk:
            inner = [None] if value.ndim == 2 else range(value.shape[0])
            entries += [(len(flat), entry) for entry in inner]
            flat.append(value)
        places.append(entries)
    return pl.pallas_call(
        functools.partial(
            tile_kernel, slots, tile, group, shard_order, gathers, scatters, places, len(flat)
        ),
        out_shape=(jax.ShapeDtypeStruct((width, rows_dev), BF16), *parts),
        in_specs=[smem, smem, smem, vmem, vmem, hbm] + [hbm] * len(flat),
        out_specs=(vmem,) * (1 + len(parts)),
        scratch_shapes=[
            pltpu.VMEM(tiles.shape, BF16),
            pltpu.VMEM((shards * block_count, width, tile), BF16),
            pltpu.VMEM((shards * block_count, width, tile), F32),
            pltpu.SemaphoreType.DMA((block_count, slots // group)),
            pltpu.SemaphoreType.DMA((shards, block_count)),
        ],
        compiler_params=pltpu.CompilerParams(vmem_limit_bytes=vmem_bytes + MIB),
        cost_estimate=pl.CostEstimate(
            flops=flops, bytes_accessed=2 * tiles.size, transcendentals=width * rows_dev
        ),
    )(
        coords.reshape(-1),
        counts,
        me.reshape(1),
        bias[:, None],
        cotangent,
        *[in_hbm(v) for v in (tiles, *flat)],
    )


def in_vmem(value):
    return pltpu.with_memory_space_constraint(value, pltpu.VMEM)


def in_hbm(value):
    return pltpu.with_memory_space_constraint(value, pltpu.HBM)


SMEM = pl.BlockSpec(memory_space=pltpu.SMEM)
VMEM = pl.BlockSpec(memory_space=pltpu.VMEM)
ANY = pl.BlockSpec(memory_space=pl.ANY)


def small_call(kernel, out_shape, values, after, pinned=True, scalars=()):
    outs = jax.tree.leaves(out_shape)
    touched = sum(v.size * v.dtype.itemsize for v in (*values, *outs))
    return pl.pallas_call(
        kernel,
        out_shape=out_shape,
        in_specs=[SMEM] * len(scalars) + [VMEM] * len(values) + [ANY] * len(after),
        out_specs=jax.tree.map(lambda _: VMEM, out_shape),
        compiler_params=pltpu.CompilerParams(vmem_limit_bytes=2 * touched + 2 * MIB),
        cost_estimate=pl.CostEstimate(flops=0, bytes_accessed=0, transcendentals=0),
    )(*scalars, *[in_vmem(v) for v in values] if pinned else values, *after)


def sum_dots(lefts, rights, dims, outer, before=(), after=()):
    (left_dim,), unused_right = dims
    number = len(lefts)
    rows, cols = lefts[0].shape[1 - left_dim], rights[0][0].shape[1]
    skip = sum(v.shape[1] for v in before)
    flat = [v for right in rights for v in right]

    def kernel(outer_ref, *refs):
        total, place = None, number
        for left, right in zip(refs[:number], rights):
            value = refs[place][...]
            if len(right) > 1:
                value = jnp.where(outer_ref[0] == 1, refs[place + 1][...], value)
            place += len(right)
            term = lax.dot_general(left[...], value, (dims, ((), ())), preferred_element_type=F32)
            total = term if total is None else total + term
        start = 0
        for ref in refs[place : place + len(before)]:
            refs[-1][:, start : start + ref.shape[1]] = ref[...]
            start += ref.shape[1]
        refs[-1][:, skip:] = total.astype(BF16)

    out = jax.ShapeDtypeStruct((rows, skip + cols), BF16)
    return small_call(kernel, out, (*lefts, *flat, *before), after, False, (outer,))


def pack(values):
    out = jax.ShapeDtypeStruct((len(values),) + values[0].shape, values[0].dtype)

    def kernel(*refs):
        for j, ref in enumerate(refs[:-1]):
            refs[-1][j] = ref[...]

    return small_call(kernel, out, values, (), False)


def add_up(values, dtype, after=()):
    number = len(values)

    def kernel(*refs):
        total = None
        for ref in refs[:number]:
            value = (ref[0] if len(ref.shape) == 3 else ref[...]).astype(F32)
            total = value if total is None else total + value
        refs[-1][...] = total.astype(dtype)

    out = jax.ShapeDtypeStruct(values[0].shape[-2:], dtype)
    return small_call(kernel, out, values, after)


def chip_sums(keep, got, after=()):
    number = keep.shape[0] - 1

    def kernel(keep_ref, got_ref, *refs):
        for j, out_ref in enumerate(refs[len(after) :], 1):
            out_ref[...] = (keep_ref[j].astype(F32) + got_ref[j].astype(F32)).astype(BF16)

    out = (jax.ShapeDtypeStruct(keep.shape[1:], BF16),) * number
    return small_call(kernel, out, (keep, got), after)


def weight_parts(scale, cols_order, rows_order, col, me, outer, grads, x_parts, after=()):
    width = grads[0].shape[0]
    rows_dev = sum(g.shape[1] for g in grads)
    n_rows = len(rows_order)
    half = n_rows // 2
    rows_out = width * len(cols_order) // n_rows
    values = (*grads, *[v for parts in x_parts for choice in parts for v in choice])

    def kernel(col_ref, me_ref, outer_ref, *refs):
        keep_ref, send_ref, grad, xs, part, sems = refs[-6:]
        always, chosen, place = [], ([], []), 0

        def copy_to(target, start):
            nonlocal place
            source = refs[place]
            lanes = pl.ds(start, source.shape[1])
            copy = pltpu.make_async_copy(source, target.at[:, lanes], sems.at[place])
            place += 1
            return copy

        start = 0
        for value in grads:
            always.append(copy_to(grad, start))
            start += value.shape[1]
        for j, parts in enumerate(x_parts):
            start = 0
            for choice in parts:
                copies = [copy_to(xs.at[j], start) for unused in choice]
                if len(copies) == 1:
                    always += copies
                else:
                    for group, copy in zip(chosen, copies):
                        group.append(copy)
                start += choice[0].shape[1]
        for copy in always:
            copy.start()
        for flag, group in enumerate(chosen):
            if group:

                @pl.when(outer_ref[0] == flag)
                def _():
                    for copy in group:
                        copy.start()
                    for copy in group:
                        copy.wait()

        for copy in always:
            copy.wait()
        for j, k in enumerate(cols_order):
            start = pl.multiple_of((col_ref[0] ^ k) * width, 16)
            product = lax.dot_general(
                xs[j], grad[...], (((1,), (1,)), ((), ())), preferred_element_type=F32
            )
            part[pl.ds(start, width), :] = product * scale
        for j, k in enumerate(rows_order):
            start = pl.multiple_of((me_ref[0] ^ k) * rows_out, 8)
            value = part[pl.ds(start, rows_out), :]
            if j < half:
                keep_ref[j] = value
            else:
                send_ref[j - half] = value.astype(BF16)

    touched = 2 * width * rows_dev * (len(cols_order) + 1) + 8 * width * width * len(cols_order)
    return pl.pallas_call(
        kernel,
        out_shape=(
            jax.ShapeDtypeStruct((half, rows_out, width), F32),
            jax.ShapeDtypeStruct((half, rows_out, width), BF16),
        ),
        in_specs=[SMEM] * 3 + [ANY] * (len(values) + len(after)),
        out_specs=(VMEM,) * 2,
        scratch_shapes=[
            pltpu.VMEM((width, rows_dev), BF16),
            pltpu.VMEM((len(cols_order), width, rows_dev), BF16),
            pltpu.VMEM((width * len(cols_order), width), F32),
            pltpu.SemaphoreType.DMA((len(values),)),
        ],
        compiler_params=pltpu.CompilerParams(vmem_limit_bytes=2 * touched + 2 * MIB),
        cost_estimate=pl.CostEstimate(flops=0, bytes_accessed=0, transcendentals=0),
    )(col.reshape(1), me.reshape(1), outer, *values, *after)


def swap(value, axis, k):
    return lax.ppermute(value, axis, [(i, i ^ k) for i in range(lax.axis_size(axis))])


def local(features, weight, bias, tile_values, tile_coords, tile_counts, cotangent):
    rows_dev, width = features.shape
    n_rows, n_cols = lax.axis_size("rows"), lax.axis_size("cols")
    me, col = lax.axis_index("rows"), lax.axis_index("cols")
    simple = all(n > 1 and n & (n - 1) == 0 for n in (n_rows, n_cols)) and n_rows > 2
    if not simple or width * n_cols % (8 * n_rows) or width % 16:
        return local_any(features, weight, bias, tile_values, tile_coords, tile_counts, cotangent)
    cols_order = tuple(range(n_cols))
    chips = tuple(range(0, n_rows, 2))
    block_count, unused_slots, tile, unused_side = tile_values.shape
    small = block_count // 2
    gathers = (block_count,)
    scatters = (block_count,)

    line = n_cols == 4
    outer = ((col == 0) | (col == n_cols - 1)).astype(jnp.int32).reshape(1)

    def over_cols(value):
        if not line:
            return [(value,)] + [(swap(value, "cols", k),) for k in cols_order[1:]]
        far = swap(value, "cols", 2)
        across = lax.ppermute(value, "cols", [(1, 2), (2, 1)])
        near = swap(value, "cols", 1)
        return [(value,), (near,), (far,), (across, swap(far, "cols", 1))]

    x = features.T
    x_parts, start = [], 0
    for count in gathers:
        piece = x if len(gathers) == 1 else x[:, start * tile : (start + count) * tile]
        start += count
        x_parts.append(over_cols(piece))
    weight_down = [
        lax.dynamic_slice(weight, ((col ^ k) * width, col * width), (width, width))
        for k in cols_order
    ]
    weight_across = [
        lax.dynamic_slice(weight, (col * width, (col ^ k) * width), (width, width))
        for k in cols_order
    ]

    order = tuple(k + c for c in (0, 1) for k in chips)
    shards = []
    for parts in x_parts:
        hidden = sum_dots(weight_down, parts, ((0,), (0,)), outer)
        own = [hidden] + [swap(hidden, "rows", k) for k in chips[1:]]
        shards.append(own + [swap(part, "rows", 1) for part in own])

    act, *part = tile_products(
        order,
        gathers,
        scatters,
        shards,
        tile_coords,
        tile_counts,
        me,
        bias,
        cotangent.T,
        tile_values,
    )

    grads, arrived, input_grad = [], (), ()
    for c in range(len(scatters)):
        keep, send = part[2 * c : 2 * c + 2]
        got = swap(send, "rows", 1)
        sums = chip_sums(keep, got, arrived)
        arrived = tuple(swap(v, "rows", k) for v, k in zip(sums, chips[1:]))
        grad = add_up((keep, got, *arrived), BF16)
        grads.append(over_cols(grad))

    keep, send = weight_parts(
        1.0 / math.sqrt(rows_dev * n_rows),
        cols_order,
        order,
        col,
        me,
        outer,
        [g[0][0] for g in grads],
        list(zip(*x_parts)),
        tuple(grads[0][1]),
    )
    got = swap(send, "rows", 1)
    sums = chip_sums(keep, got)
    weight_grad = add_up((keep, got, *[swap(v, "rows", k) for v, k in zip(sums, chips[1:])]), F32)

    for c, values in enumerate(grads):
        last = (weight_grad,) if c + 1 == len(grads) else ()
        input_grad = (sum_dots(weight_across, values, ((1,), (0,)), outer, input_grad, last),)
    return (act.T, input_grad[0].T, weight_grad)


def contract_first(a, b):
    return lax.dot_general(a, b, (((0,), (0,)), ((), ())), preferred_element_type=F32)


def local_any(features, weight, bias, tile_values, tile_coords, tile_counts, cotangent):
    rows_dev, col_width = features.shape
    n_rows = lax.axis_size("rows")
    col_start = lax.axis_index("cols") * col_width
    x_full = lax.all_gather(features.T, "cols", axis=0, tiled=True)
    w_cols = lax.dynamic_slice_in_dim(weight, col_start, col_width, 1)
    hidden = contract_first(w_cols, x_full).astype(BF16)
    all_hidden = lax.all_gather(hidden, "rows", axis=0)
    order = tuple(range(n_rows))
    act, keep, send = tile_products(
        order,
        (tile_values.shape[0],),
        (tile_values.shape[0],),
        [[all_hidden[s] for s in order]],
        tile_coords,
        tile_counts,
        jnp.zeros((), jnp.int32),
        bias,
        cotangent.T,
        tile_values,
    )
    part = jnp.concatenate([keep, send], axis=0)
    grad_hidden = lax.psum_scatter(part, "rows", scatter_dimension=0, tiled=False)
    w_rows = lax.dynamic_slice_in_dim(weight, col_start, col_width, 0)
    grad_full = lax.all_gather(grad_hidden, "cols", axis=0, tiled=True)
    input_grad = jnp.dot(w_rows, grad_full, preferred_element_type=F32).astype(BF16)
    scale_factor = 1.0 / math.sqrt(rows_dev * n_rows)
    weight_part_sum = lax.dot_general(
        x_full, grad_hidden, (((1,), (1,)), ((), ())), preferred_element_type=F32
    )
    weight_grad = lax.psum_scatter(
        weight_part_sum * scale_factor, "rows", scatter_dimension=0, tiled=True
    )
    return (act.T, input_grad.T, weight_grad)


def solution(mesh):
    return jax.shard_map(
        local,
        mesh=mesh,
        in_specs=(
            P("rows", "cols"),
            P(),
            P("cols"),
            P("rows", None, None, None),
            P("rows", None),
            P("rows"),
            P("rows", "cols"),
        ),
        out_specs=(P("rows", "cols"), P("rows", "cols"), P("rows", "cols")),
        check_vma=False,
    )
```

```python
import functools
import math

import jax
import jax.numpy as jnp
from jax import lax
from jax.experimental import pallas as pl
from jax.experimental.pallas import tpu as pltpu
from jax.sharding import PartitionSpec as P

F32 = jnp.float32
BF16 = jnp.bfloat16
CHUNK = 16
MIB = 1024 * 1024


def largest_divisor(number, limit):
    return max(d for d in range(1, limit + 1) if number % d == 0)


def tile_kernel(
    slots,
    tile,
    group,
    shard_order,
    gathers,
    scatters,
    coords_ref,
    counts_ref,
    me_ref,
    bias_ref,
    cotangent_ref,
    tiles_ref,
    *rest,
):
    shards, block_count = len(shard_order), sum(gathers)
    hidden_refs, rest = rest[: shards * len(gathers)], rest[shards * len(gathers) :]
    act_ref, *part_refs = rest[:-5]
    tiles, hidden, partial, tile_sems, hidden_sems = rest[-5:]
    groups = slots // group
    me = me_ref[0]
    width = act_ref.shape[0]

    def tile_copy(i, q):
        span = pl.ds(q * group, group)
        return pltpu.make_async_copy(
            tiles_ref.at[i, span], tiles.at[i, span], tile_sems.at[i, q]
        )

    hidden_copies = []
    for s in range(shards):
        owner = me ^ shard_order[s]
        block = 0
        for c, count in enumerate(gathers):
            for b in range(count):
                hidden_copies.append(
                    pltpu.make_async_copy(
                        hidden_refs[c * shards + s].at[:, pl.ds(b * tile, tile)],
                        hidden.at[owner * block_count + block],
                        hidden_sems.at[s, block],
                    )
                )
                block += 1
    for copy in hidden_copies:
        copy.start()
    for i in range(block_count):
        for q in range(groups):

            @pl.when(q * group < counts_ref[i])
            def _():
                tile_copy(i, q).start()

    partial[...] = jnp.zeros_like(partial)
    for copy in hidden_copies:
        copy.wait()

    chunk = largest_divisor(slots, CHUNK)

    def several(i, p):
        parts, places = [], []
        for t in range(chunk):
            k = p * chunk + t
            value = tiles[i, k]
            if t:
                value = jnp.where(k < counts_ref[i], value, jnp.zeros_like(value))
            parts.append(value)
            places.append(coords_ref[i * slots + k])
        return jnp.concatenate(parts, axis=1), places

    for i in range(block_count):
        for q in range(groups):

            @pl.when(q * group < counts_ref[i])
            def _():
                tile_copy(i, q).wait()

        steps = (counts_ref[i] + (chunk - 1)) // chunk
        lanes = pl.ds(i * tile, tile)

        def forward(p, total):
            values, places = several(i, p)
            panel = jnp.concatenate([hidden[c] for c in places], axis=1)
            return total + lax.dot_general(
                panel, values, (((1,), (1,)), ((), ())), preferred_element_type=F32
            )

        total = lax.fori_loop(0, steps, forward, jnp.zeros((width, tile), F32))
        pre = total + bias_ref[...]
        s = jax.nn.sigmoid(pre)
        act_ref[:, lanes] = (pre * s).astype(BF16)
        slope = s * (1.0 + pre * (1.0 - s))
        grad = (cotangent_ref[:, lanes].astype(F32) * slope).astype(BF16)

        def backward(p, carry):
            values, places = several(i, p)
            out = jnp.dot(grad, values, preferred_element_type=F32)
            for t, c in enumerate(places):
                partial[c] += out[:, t * tile : (t + 1) * tile]
            return carry

        lax.fori_loop(0, steps, backward, 0)

    half = shards // 2
    first = 0
    for c, count in enumerate(scatters):
        keep_own, keep, send_own, send = part_refs[4 * c : 4 * c + 4]
        for s in range(shards):
            own, others = (keep_own, keep) if s < half else (send_own, send)
            out_ref = own if s % half == 0 else others.at[s % half - 1]
            owner = me ^ shard_order[s]
            for b in range(count):
                value = partial[owner * block_count + first + b].astype(BF16)
                out_ref[:, b * tile : (b + 1) * tile] = value
        first += count


def tile_products(
    shard_order, gathers, scatters, hidden, coords, counts, me, bias, cotangent, tiles
):
    block_count, slots, tile, unused_side = tiles.shape
    width, rows_dev = cotangent.shape
    shards = len(shard_order)
    group = largest_divisor(slots, 8)
    smem = pl.BlockSpec(memory_space=pltpu.SMEM)
    vmem = pl.BlockSpec(memory_space=pltpu.VMEM)
    hbm = pl.BlockSpec(memory_space=pltpu.HBM)
    vmem_bytes = 2 * tiles.size + (6 + 2) * shards * width * rows_dev + 16 * cotangent.size
    flops = 4 * block_count * slots * tile * tile * width
    parts = []
    for count in scatters:
        own = jax.ShapeDtypeStruct((width, count * tile), BF16)
        others = jax.ShapeDtypeStruct((max(shards // 2 - 1, 1), width, count * tile), BF16)
        parts += [own, others] * 2
    flat = [v for chunk in hidden for v in chunk]
    return pl.pallas_call(
        functools.partial(tile_kernel, slots, tile, group, shard_order, gathers, scatters),
        out_shape=(jax.ShapeDtypeStruct((width, rows_dev), BF16), *parts),
        in_specs=[smem, smem, smem, vmem, vmem, hbm] + [hbm] * len(flat),
        out_specs=(vmem,) * (1 + len(parts)),
        scratch_shapes=[
            pltpu.VMEM(tiles.shape, BF16),
            pltpu.VMEM((shards * block_count, width, tile), BF16),
            pltpu.VMEM((shards * block_count, width, tile), F32),
            pltpu.SemaphoreType.DMA((block_count, slots // group)),
            pltpu.SemaphoreType.DMA((shards, block_count)),
        ],
        compiler_params=pltpu.CompilerParams(vmem_limit_bytes=vmem_bytes + MIB),
        cost_estimate=pl.CostEstimate(
            flops=flops, bytes_accessed=2 * tiles.size, transcendentals=width * rows_dev
        ),
    )(
        coords.reshape(-1),
        counts,
        me.reshape(1),
        bias[:, None],
        cotangent,
        *[in_hbm(v) for v in (tiles, *flat)],
    )


def in_vmem(value):
    return pltpu.with_memory_space_constraint(value, pltpu.VMEM)


def in_hbm(value):
    return pltpu.with_memory_space_constraint(value, pltpu.HBM)


VMEM = pl.BlockSpec(memory_space=pltpu.VMEM)
ANY = pl.BlockSpec(memory_space=pl.ANY)


def small_call(kernel, out_shape, values, after, pinned=True):
    outs = jax.tree.leaves(out_shape)
    touched = sum(v.size * v.dtype.itemsize for v in (*values, *outs))
    return pl.pallas_call(
        kernel,
        out_shape=out_shape,
        in_specs=[VMEM] * len(values) + [ANY] * len(after),
        out_specs=jax.tree.map(lambda _: VMEM, out_shape),
        compiler_params=pltpu.CompilerParams(vmem_limit_bytes=2 * touched + 2 * MIB),
        cost_estimate=pl.CostEstimate(flops=0, bytes_accessed=0, transcendentals=0),
    )(*[in_vmem(v) for v in values] if pinned else values, *after)


def sum_dots(lefts, rights, dims, before=(), after=()):
    (left_dim,), unused_right = dims
    number = len(lefts)
    rows, cols = lefts[0].shape[1 - left_dim], rights[0].shape[1]
    skip = sum(v.shape[1] for v in before)

    def kernel(*refs):
        total = None
        for left, right in zip(refs[:number], refs[number : 2 * number]):
            term = lax.dot_general(
                left[...], right[...], (dims, ((), ())), preferred_element_type=F32
            )
            total = term if total is None else total + term
        start = 0
        for ref in refs[2 * number : 2 * number + len(before)]:
            refs[-1][:, start : start + ref.shape[1]] = ref[...]
            start += ref.shape[1]
        refs[-1][:, skip:] = total.astype(BF16)

    out = jax.ShapeDtypeStruct((rows, skip + cols), BF16)
    return small_call(kernel, out, (*lefts, *rights, *before), after, False)


def add_up(values, dtype, after=()):
    number = len(values)

    def kernel(*refs):
        total = None
        for ref in refs[:number]:
            value = (ref[0] if len(ref.shape) == 3 else ref[...]).astype(F32)
            total = value if total is None else total + value
        refs[-1][...] = total.astype(dtype)

    out = jax.ShapeDtypeStruct(values[0].shape[-2:], dtype)
    return small_call(kernel, out, values, after)


def chip_sums(keep, got, after=(), first=0):
    number = keep.shape[0] - first

    def kernel(keep_ref, got_ref, *refs):
        for j, out_ref in enumerate(refs[len(after) :], first):
            out_ref[...] = (keep_ref[j].astype(F32) + got_ref[j].astype(F32)).astype(BF16)

    out = (jax.ShapeDtypeStruct(keep.shape[1:], BF16),) * number
    return small_call(kernel, out, (keep, got), after)


def weight_parts(scale, cols_order, rows_order, col, me, grads, x_parts, after=()):
    width = grads[0].shape[0]
    rows_dev = sum(g.shape[1] for g in grads)
    n_rows = len(rows_order)
    half = n_rows // 2
    rows_out = width * len(cols_order) // n_rows
    pieces = len(x_parts[0])
    values = (*grads, *[p for parts in x_parts for p in parts])

    def kernel(col_ref, me_ref, *refs):
        inputs = refs[: len(values)]
        keep_ref, send_ref, grad, xs, part, sems = refs[-6:]
        copies = []

        def fill(target, sources, first_sem):
            start = 0
            for j, source in enumerate(sources):
                lanes = pl.ds(start, source.shape[1])
                copy = pltpu.make_async_copy(source, target.at[:, lanes], sems.at[first_sem + j])
                copy.start()
                copies.append(copy)
                start += source.shape[1]

        fill(grad, inputs[: len(grads)], 0)
        for j in range(len(cols_order)):
            first = len(grads) + j * pieces
            fill(xs.at[j], inputs[first : first + pieces], first)
        for copy in copies:
            copy.wait()
        for j, k in enumerate(cols_order):
            start = pl.multiple_of((col_ref[0] ^ k) * width, 16)
            product = lax.dot_general(
                xs[j], grad[...], (((1,), (1,)), ((), ())), preferred_element_type=F32
            )
            part[pl.ds(start, width), :] = product * scale
        for j, k in enumerate(rows_order):
            start = pl.multiple_of((me_ref[0] ^ k) * rows_out, 8)
            value = part[pl.ds(start, rows_out), :]
            if j < half:
                keep_ref[j] = value
            else:
                send_ref[j - half] = value.astype(BF16)

    touched = 2 * width * rows_dev * (len(cols_order) + 1) + 8 * width * width * len(cols_order)
    smem = pl.BlockSpec(memory_space=pltpu.SMEM)
    return pl.pallas_call(
        kernel,
        out_shape=(
            jax.ShapeDtypeStruct((half, rows_out, width), F32),
            jax.ShapeDtypeStruct((half, rows_out, width), BF16),
        ),
        in_specs=[smem, smem] + [ANY] * (len(values) + len(after)),
        out_specs=(VMEM,) * 2,
        scratch_shapes=[
            pltpu.VMEM((width, rows_dev), BF16),
            pltpu.VMEM((len(cols_order), width, rows_dev), BF16),
            pltpu.VMEM((width * len(cols_order), width), F32),
            pltpu.SemaphoreType.DMA((len(values),)),
        ],
        compiler_params=pltpu.CompilerParams(vmem_limit_bytes=2 * touched + 2 * MIB),
        cost_estimate=pl.CostEstimate(flops=0, bytes_accessed=0, transcendentals=0),
    )(col.reshape(1), me.reshape(1), *values, *after)


def swap(value, axis, k):
    return lax.ppermute(value, axis, [(i, i ^ k) for i in range(lax.axis_size(axis))])


def local(features, weight, bias, tile_values, tile_coords, tile_counts, cotangent):
    rows_dev, width = features.shape
    n_rows, n_cols = lax.axis_size("rows"), lax.axis_size("cols")
    me, col = lax.axis_index("rows"), lax.axis_index("cols")
    simple = all(n > 1 and n & (n - 1) == 0 for n in (n_rows, n_cols)) and n_rows > 2
    if not simple or width * n_cols % (8 * n_rows) or width % 16:
        return local_any(features, weight, bias, tile_values, tile_coords, tile_counts, cotangent)
    cols_order = tuple(range(n_cols))
    chips = tuple(range(0, n_rows, 2))
    block_count, unused_slots, tile, unused_side = tile_values.shape
    small = block_count // 2
    gathers = (block_count - small, small) if small else (block_count,)
    scatters = gathers[::-1]

    x = features.T
    x_parts, start = [], 0
    for count in gathers:
        piece = x[:, start * tile : (start + count) * tile]
        x_parts.append([piece] + [swap(piece, "cols", k) for k in cols_order[1:]])
        start += count
    weight_down = [
        lax.dynamic_slice(weight, ((col ^ k) * width, col * width), (width, width))
        for k in cols_order
    ]
    weight_across = [
        lax.dynamic_slice(weight, (col * width, (col ^ k) * width), (width, width))
        for k in cols_order
    ]

    order = tuple(k + c for c in (0, 1) for k in chips)
    shards = []
    for parts in x_parts:
        hidden = sum_dots(weight_down, parts, ((0,), (0,)))
        own = [hidden] + [swap(hidden, "rows", k) for k in chips[1:]]
        shards.append(own + [swap(part, "rows", 1) for part in own])

    act, *part = tile_products(
        order,
        gathers,
        scatters,
        shards,
        tile_coords,
        tile_counts,
        me,
        bias,
        cotangent.T,
        tile_values,
    )

    grads, arrived, input_grad = [], (), ()
    for c in range(len(scatters)):
        keep_own, keep, send_own, send = part[4 * c : 4 * c + 4]
        got, got_own = swap(send, "rows", 1), swap(send_own, "rows", 1)
        sums = chip_sums(keep, got, arrived)
        arrived = tuple(swap(v, "rows", k) for v, k in zip(sums, chips[1:]))
        grad = add_up((keep_own, got_own, *arrived), BF16)
        grads.append([grad] + [swap(grad, "cols", k) for k in cols_order[1:]])

    keep, send = weight_parts(
        1.0 / math.sqrt(rows_dev * n_rows),
        cols_order,
        order,
        col,
        me,
        [g[0] for g in grads],
        list(zip(*x_parts)),
        tuple(grads[0][1:]) if len(grads) > 1 else (),
    )
    got = swap(send, "rows", 1)
    sums = chip_sums(keep, got, first=1)
    weight_grad = add_up((keep, got, *[swap(v, "rows", k) for v, k in zip(sums, chips[1:])]), F32)

    for c, values in enumerate(grads):
        last = (weight_grad,) if c + 1 == len(grads) else ()
        input_grad = (sum_dots(weight_across, values, ((1,), (0,)), input_grad, last),)
    return (act.T, input_grad[0].T, weight_grad)


def contract_first(a, b):
    return lax.dot_general(a, b, (((0,), (0,)), ((), ())), preferred_element_type=F32)


def local_any(features, weight, bias, tile_values, tile_coords, tile_counts, cotangent):
    rows_dev, col_width = features.shape
    n_rows = lax.axis_size("rows")
    col_start = lax.axis_index("cols") * col_width
    x_full = lax.all_gather(features.T, "cols", axis=0, tiled=True)
    w_cols = lax.dynamic_slice_in_dim(weight, col_start, col_width, 1)
    hidden = contract_first(w_cols, x_full).astype(BF16)
    all_hidden = lax.all_gather(hidden, "rows", axis=0)
    order = tuple(range(n_rows))
    act, keep_own, keep, send_own, send = tile_products(
        order,
        (tile_values.shape[0],),
        (tile_values.shape[0],),
        [[all_hidden[s] for s in order]],
        tile_coords,
        tile_counts,
        jnp.zeros((), jnp.int32),
        bias,
        cotangent.T,
        tile_values,
    )
    part = jnp.concatenate([keep_own[None], keep, send_own[None], send], axis=0)
    grad_hidden = lax.psum_scatter(part, "rows", scatter_dimension=0, tiled=False)
    w_rows = lax.dynamic_slice_in_dim(weight, col_start, col_width, 0)
    grad_full = lax.all_gather(grad_hidden, "cols", axis=0, tiled=True)
    input_grad = jnp.dot(w_rows, grad_full, preferred_element_type=F32).astype(BF16)
    scale_factor = 1.0 / math.sqrt(rows_dev * n_rows)
    weight_part_sum = lax.dot_general(
        x_full, grad_hidden, (((1,), (1,)), ((), ())), preferred_element_type=F32
    )
    weight_grad = lax.psum_scatter(
        weight_part_sum * scale_factor, "rows", scatter_dimension=0, tiled=True
    )
    return (act.T, input_grad.T, weight_grad)


def solution(mesh):
    return jax.shard_map(
        local,
        mesh=mesh,
        in_specs=(
            P("rows", "cols"),
            P(),
            P("cols"),
            P("rows", None, None, None),
            P("rows", None),
            P("rows"),
            P("rows", "cols"),
        ),
        out_specs=(P("rows", "cols"), P("rows", "cols"), P("rows", "cols")),
        check_vma=False,
    )
```
